256 devices in a mesh: dp: 8 (over y, x_lo), shard: 32 (over x_hi, z, core).
Axes of the slice: x: 4 (x_hi: 2, x_lo: 2; x = x_hi * 2 + x_lo), y: 4, z: 8, core: 2. Of those that a mesh axis runs over, the one named last changes fastest.
Arguments:
- grad_parts: bfloat16 [8, 96, 512, 2048], P('dp', None, 'shard'), may hold values from -40 to 40
- momentum: float32 [96, 512, 2048], P('dp', 'shard'), may hold values from -8 to 8
- weight: bfloat16 [96, 512, 2048], P('dp', 'shard'), may hold values from -4 to 4
Outputs:
- new_momentum: float32 [96, 512, 2048], P('dp', 'shard')
- update: float32 [96, 512, 2048], P('dp', 'shard')
- new_weight: bfloat16 [96, 512, 2048], P('dp', 'shard')
The draws below stay inside these ranges and needn't reach their ends.
All inputs are finite; a program needn't handle non-finite values.
Results may differ from the reference program's by a relative error of at most 0.02.
Values may be sent and summed in bfloat16 or wider, within the bound.
A program may use at most 128 MiB of HBM per device.

```python
import math
import jax
import jax.numpy as jnp
from jax import lax

ROWS = 512
COLS = 2048
ITERS = 5
MATS = 96
N_DP = 8


def draw_grad_parts(key, part):
    first, second, third = jax.random.split(jax.random.fold_in(key, 17), 3)
    shape = (N_DP, MATS, ROWS, COLS)
    ramp = jnp.exp(math.log(3.0) * jnp.arange(ROWS, dtype=jnp.float32) / ROWS)
    row_scale = jnp.exp(jax.random.uniform(second, (MATS, ROWS, 1), jnp.float32, math.log(0.3), math.log(3.0))) * ramp[None, :, None]
    col_scale = jnp.exp(jax.random.uniform(third, (MATS, 1, COLS), jnp.float32, math.log(0.3), math.log(3.0)))
    values = jnp.clip(jax.random.normal(first, shape, jnp.float32), -4.0, 4.0)
    return jnp.clip(values * row_scale[None] * col_scale[None], -40.0, 40.0).astype(jnp.bfloat16)


def block_scale(own_key, dims, cuts, least, top_value):
    level = 1.0
    for position, blocks in cuts:
        heights = jax.random.uniform(jax.random.fold_in(jax.random.fold_in(own_key, 6), position), (blocks,), jnp.float32, least / len(cuts), top_value / len(cuts))
        level = level * jnp.repeat(jnp.exp(heights), dims[position] // blocks).reshape((-1,) + (1,) * (len(dims) - 1 - position))
    return level


def normal_values(own_key, extent, width, limit, shards=(), held_as=jnp.bfloat16):
    entries = jax.random.normal(own_key, extent, jnp.float32) * width
    if len(shards) > 0:
        entries = block_scale(own_key, extent, shards, -0.22, 0.18) * entries
    return jnp.clip(entries, min=-limit, max=limit).astype(held_as)


def setup_inputs(seed: int = 0) -> dict:
    splits = jax.random.split(jax.random.key(seed), 4)
    grad_parts = draw_grad_parts(jax.random.fold_in(splits[3], 71), 0)
    momentum = normal_values(splits[1], (MATS, ROWS, COLS), 2.0, 8.0, ((0, 8), (1, 32)), jnp.float32)
    weight = normal_values(splits[2], (MATS, ROWS, COLS), 1.0, 4.0, ((0, 8), (1, 32)))
    return dict(grad_parts=grad_parts, momentum=momentum, weight=weight)


linear_term = 3.4445
square_term = -4.775
fourth_term = 2.0315
decay_rate = 0.95
step_size = 0.05
tiny_norm = 1e-07

def newton_schulz(start):
    current = start
    for step in range(ITERS):
        gram = lax.dot_general(current, current, (((1,), (1,)), ((), ())), preferred_element_type=jnp.float32)
        square = jnp.dot(gram, gram, preferred_element_type=jnp.float32, precision=lax.Precision.HIGHEST)
        poly = (square_term * gram + fourth_term * square).astype(jnp.bfloat16)
        current = (linear_term * current.astype(jnp.float32) + jnp.dot(poly, current, preferred_element_type=jnp.float32)).astype(jnp.bfloat16)
    return current

def reference(grad_parts, momentum, weight):
    shape_scale = 0.2 * math.sqrt(max(ROWS, COLS))

    def single(items):
        parts, moment, current = items
        gradient = lax.optimization_barrier(jnp.sum(parts.astype(jnp.float32), axis=0))
        next_moment = decay_rate * moment + gradient
        nesterov = gradient + decay_rate * next_moment
        total = jnp.sum(nesterov * nesterov)
        start = (nesterov / (jnp.sqrt(total) + tiny_norm)).astype(jnp.bfloat16)
        result = newton_schulz(start)
        scaled = shape_scale * result.astype(jnp.float32)
        fresh = (current.astype(jnp.float32) - step_size * scaled).astype(jnp.bfloat16)
        return (next_moment, scaled, fresh)
    moments, updates, weights = lax.map(single, (jnp.moveaxis(grad_parts, 1, 0), momentum, weight))
    return (moments, updates, weights)
```

```python
import functools
import math

import jax
import jax.numpy as jnp
from jax import lax
from jax.experimental import pallas as pl
from jax.experimental.pallas import tpu as pltpu
from jax.sharding import PartitionSpec as P

MESH = pl.DeviceIdType.MESH
F32 = jnp.float32
BF16 = jnp.bfloat16

MATS = 12
ROWS = 512
COLS = 2048
BAND = 16
SHARDS = 32
ITERS = 5
NA = 8
NB = MATS - NA
HB = NB // 2

CHUNKS = 8
WIDTH = COLS // CHUNKS
AHEAD = 2

linear_term = 3.4445
square_term = -4.775
fourth_term = 2.0315
decay_rate = 0.95
step_size = 0.05
tiny_norm = 1e-07

A_R, A_D, A_S, A_X, B_X, B_R, B_D, B_S = 0, 2, 4, 6, 7, 8, 10, 12
KINDS = 14


def owner_of(k):
    return 2 * ((4 * k) // 3)


def dot(a, b):
    return jnp.dot(a, b, preferred_element_type=F32)


def dot_t(a, b):
    return lax.dot_general(a, b, (((1,), (1,)), ((), ())), preferred_element_type=F32)


def poly_of(gram_ref, poly_ref, scale2):
    half = ROWS // 2
    top = gram_ref[:half, :] * scale2
    low = gram_ref[half:, half:] * scale2
    high_top = top.astype(BF16)
    rest_top = (top - high_top.astype(F32)).astype(BF16)
    high_low = low.astype(BF16)
    rest_low = (low - high_low.astype(F32)).astype(BF16)
    corner = top[:, half:].T
    high_corner = corner.astype(BF16)
    rest_corner = (corner - high_corner.astype(F32)).astype(BF16)
    high_bottom = jnp.concatenate([high_corner, high_low], axis=1)
    rest_bottom = jnp.concatenate([rest_corner, rest_low], axis=1)
    high = jnp.concatenate([high_top, high_bottom], axis=0)
    rest = jnp.concatenate([rest_top, rest_bottom], axis=0)
    cross_top = dot(high_top, rest)
    cross_bottom = dot(high_bottom, rest)
    square_top = dot(high_top, high)
    square_low = dot(high_bottom, high[:, half:])
    flipped = jnp.concatenate([cross_top[:, :half].T, cross_bottom[:, :half].T], axis=1)
    poly_top = square_term * top + fourth_term * (square_top + (cross_top + flipped))
    cross_low = cross_bottom[:, half:]
    poly_low = square_term * low + fourth_term * (square_low + (cross_low + cross_low.T))
    poly_ref[:half, :] = poly_top.astype(BF16)
    poly_ref[half:, half:] = poly_low.astype(BF16)
    poly_ref[half:, :half] = poly_top[:, half:].T.astype(BF16)


def add_gram(gram_ref, block):
    half = ROWS // 2
    gram_ref[:half, :] += dot_t(block[:half], block)
    gram_ref[half:, half:] += dot_t(block[half:], block[half:])


def clear_gram(gram_ref):
    gram_ref[...] = jnp.zeros_like(gram_ref)


NSW = 512


def orthogonalize(source, work, gram_ref, poly_ref, send):
    half = ROWS // 2
    row = lax.broadcasted_iota(jnp.int32, (half, half), 0)
    col = lax.broadcasted_iota(jnp.int32, (half, half), 1)
    diag = jnp.where(row == col, gram_ref[:half, :half] + gram_ref[half:, half:], 0.0)
    total = jnp.sum(jnp.sum(diag, axis=1, keepdims=True), axis=0, keepdims=True)
    scale = 1.0 / (jnp.sqrt(total) + tiny_norm)

    def apply(src, c, factor):
        cols = pl.ds(pl.multiple_of(c * NSW, NSW), NSW)
        block = src[:, :, cols].reshape(ROWS, NSW)
        new = linear_term * block.astype(F32) + dot(poly_ref[...], block)
        if factor is not None:
            new = new * factor
        new = new.astype(BF16)
        work[:, :, cols] = new.reshape(SHARDS, BAND, NSW)
        return new

    poly_of(gram_ref, poly_ref, scale * scale)
    clear_gram(gram_ref)

    @pl.loop(0, COLS // NSW)
    def _(c):
        add_gram(gram_ref, apply(source, c, scale))

    @pl.loop(0, ITERS - 2)
    def _(it):
        poly_of(gram_ref, poly_ref, 1.0)
        clear_gram(gram_ref)

        @pl.loop(0, COLS // NSW)
        def _(c):
            add_gram(gram_ref, apply(work, c, None))

    poly_of(gram_ref, poly_ref, 1.0)

    @pl.loop(0, COLS // NSW)
    def _(c):
        apply(work, c, None)
        send(c)


def kernel(
    grads, momentum, moment_out, ortho_out,
    own_p, own_m, own_c, own_b, a_r, a_d, a_s, a_x, a_send, ax_send,
    b_x, b_u, b_r, b_d, b_s, b_send,
    nest, gathered, work, gram_ref, poly_ref,
    load_sem, send_sem, recv_sem, gsend_sem, grecv_sem, ssend_sem, srecv_sem,
):
    dp = lax.axis_index("dp")
    me = lax.axis_index("shard")
    y, x = dp // 2, dp % 2
    other = 1 - x
    up_y, down_y, far_y = (y + 1) % 4, (y + 3) % 4, (y + 2) % 4
    up = (up_y * 2 + x, me)
    down = (down_y * 2 + x, me)
    partner = (y * 2 + other, me)
    way = (up, down)

    loads = [
        pltpu.make_async_copy(grads.at[up_y, 0, pl.ds(0, NA)], own_p, load_sem.at[0]),
        pltpu.make_async_copy(grads.at[down_y, 1, pl.ds(0, NA)], own_m, load_sem.at[1]),
        pltpu.make_async_copy(grads.at[y, :, pl.ds(0, NA)], own_c, load_sem.at[2]),
        pltpu.make_async_copy(grads.at[:, x, pl.ds(NA, NB)], own_b, load_sem.at[3]),
    ]
    for load in loads:
        load.start()

    barrier = pltpu.get_barrier_semaphore()
    for device in (up, down, partner):
        pl.semaphore_signal(barrier, inc=1, device_id=device, device_id_type=MESH)

    @pl.loop(1, SHARDS)
    def _(r):
        pl.semaphore_signal(barrier, inc=1, device_id=(dp, (me + r) % SHARDS), device_id_type=MESH)

    pl.semaphore_wait(barrier, 3 + SHARDS - 1)

    for load in loads:
        load.wait()

    def columns(c):
        return pl.ds(pl.multiple_of(c * WIDTH, WIDTH), WIDTH)

    def message(kind, c, src, dst, device):
        return pltpu.make_async_remote_copy(
            src_ref=src, dst_ref=dst, send_sem=send_sem.at[kind, c], recv_sem=recv_sem.at[kind, c],
            device_id=device, device_id_type=MESH,
        )

    def a_relay(g, c):
        cols = columns(c)
        return message(A_R + g, c, grads.at[far_y, g, pl.ds(0, NA), :, cols], a_r.at[g, :, :, cols], way[g])

    def a_direct(g, c):
        cols = columns(c)
        target = (down_y, up_y)[g]
        return message(A_D + g, c, grads.at[target, g, pl.ds(0, NA), :, cols], a_d.at[g, :, :, cols], way[1 - g])

    def a_sum(g, c):
        cols = columns(c)
        return message(A_S + g, c, a_send.at[g, :, :, cols], a_s.at[g, :, :, cols], way[g])

    def a_cross(c):
        cols = columns(c)
        return message(A_X, c, ax_send.at[:, :, cols], a_x.at[:, :, cols], partner)

    def b_cross(c):
        cols = columns(c)
        return message(B_X, c, grads.at[:, other, pl.ds(NA, NB), :, cols], b_x.at[:, :, :, cols], partner)

    def b_relay(g, c):
        cols = columns(c)
        return message(B_R + g, c, b_u.at[far_y, pl.ds(g * HB, HB), :, cols], b_r.at[g, :, :, cols], way[g])

    def b_direct(g, c):
        cols = columns(c)
        target = (down_y, up_y)[g]
        return message(B_D + g, c, b_u.at[target, pl.ds(g * HB, HB), :, cols], b_d.at[g, :, :, cols], way[1 - g])

    def b_sum(g, c):
        cols = columns(c)
        return message(B_S + g, c, b_send.at[g, :, :, cols], b_s.at[g, :, :, cols], way[g])

    def issue(c):
        b_cross(c).start()
        for g in (0, 1):
            a_relay(g, c).start()
        for g in (0, 1):
            a_direct(g, c).start()

    def stage1(c):
        cols = columns(c)
        own = (own_p, own_m)
        for g in (0, 1):
            a_relay(g, c).wait_recv()
            total = own[g][:, :, cols].astype(F32) + a_r[g, :, :, cols].astype(F32)
            a_send[g, :, :, cols] = total.astype(BF16)
            a_sum(g, c).start()
        b_cross(c).wait_recv()
        for t in range(4):
            total = own_b[t, :, :, cols].astype(F32) + b_x[t, :, :, cols].astype(F32)
            b_u[t, :, :, cols] = total.astype(BF16)
        for g in (0, 1):
            b_relay(g, c).start()
        for g in (0, 1):
            b_direct(g, c).start()

    def a_total(g, c):
        cols = columns(c)
        return own_c[g, :, :, cols].astype(F32) + a_d[g, :, :, cols].astype(F32) + a_s[g, :, :, cols].astype(F32)

    def stage2(c):
        cols = columns(c)
        for g in (0, 1):
            a_direct(g, c).wait_recv()
            a_sum(g, c).wait_recv()
        ax_send[:, :, cols] = a_total(other, c).astype(BF16)
        a_cross(c).start()
        own = (up_y, down_y)
        for g in (0, 1):
            b_relay(g, c).wait_recv()
            mine = own_b[own[g], g * HB:(g + 1) * HB, :, cols].astype(F32)
            crossed = b_x[own[g], g * HB:(g + 1) * HB, :, cols].astype(F32)
            b_send[g, :, :, cols] = (mine + crossed + b_r[g, :, :, cols].astype(F32)).astype(BF16)
            b_sum(g, c).start()

    def finish(first, gradient, cols):
        count = gradient.shape[0]
        moment = decay_rate * momentum[first:first + count, :, cols] + gradient
        moment_out[first:first + count, :, cols] = moment
        nest[first:first + count, :, cols] = (gradient + decay_rate * moment).astype(BF16)

    def to_owner(k, c):
        cols = columns(c)
        return pltpu.make_async_remote_copy(
            src_ref=nest.at[k, :, cols], dst_ref=gathered.at[me, :, cols],
            send_sem=gsend_sem.at[k], recv_sem=grecv_sem.at[c],
            device_id=(dp, owner_of(k)), device_id_type=MESH,
        )

    def stage3(c):
        cols = columns(c)
        for g in (0, 1):
            b_direct(g, c).wait_recv()
            b_sum(g, c).wait_recv()
            mine = own_b[y, g * HB:(g + 1) * HB, :, cols].astype(F32)
            crossed = b_x[y, g * HB:(g + 1) * HB, :, cols].astype(F32)
            arrived = b_d[g, :, :, cols].astype(F32) + b_s[g, :, :, cols].astype(F32)
            finish(NA + g * HB, mine + crossed + arrived, cols)
        a_cross(c).wait_recv()
        finish(0, a_total(x, c) + a_x[:, :, cols].astype(F32), cols)

        @pl.loop(0, MATS)
        def _(k):
            mine = owner_of(k) == me

            @pl.when(mine)
            def _():
                pltpu.make_async_copy(nest.at[k, :, cols], gathered.at[me, :, cols], grecv_sem.at[c]).start()

            @pl.when(jnp.logical_not(mine))
            def _():
                to_owner(k, c).start()

    for c in range(AHEAD):
        issue(c)

    def guarded(step, offset, stage):
        @pl.when(jnp.logical_and(step >= offset, step < CHUNKS + offset))
        def _():
            stage(step - offset)

    @pl.loop(0, CHUNKS + 2)
    def _(step):
        guarded(step, 0, stage1)
        guarded(step, 1, stage2)
        guarded(step, 2, stage3)
        guarded(step, -AHEAD, issue)

    chip = me // 2
    slot = (3 * chip + 3) // 4
    is_owner = jnp.logical_and(me % 2 == 0, chip % 4 != 3)

    @pl.when(is_owner)
    def _():
        clear_gram(gram_ref)

        @pl.loop(0, CHUNKS)
        def _(c):
            cols = columns(c)
            whole = gathered.at[:, :, cols]
            pltpu.make_async_copy(whole, whole, grecv_sem.at[c]).wait()
            add_gram(gram_ref, gathered[:, :, cols].reshape(ROWS, WIDTH))

        def scatter(c):
            cols = pl.ds(pl.multiple_of(c * NSW, NSW), NSW)
            pltpu.make_async_copy(work.at[me, :, cols], ortho_out.at[slot, :, cols], srecv_sem.at[slot]).start()

            @pl.loop(1, SHARDS)
            def _(r):
                to = (me + r) % SHARDS
                pltpu.make_async_remote_copy(
                    src_ref=work.at[to, :, cols], dst_ref=ortho_out.at[slot, :, cols],
                    send_sem=ssend_sem.at[c], recv_sem=srecv_sem.at[slot],
                    device_id=(dp, to), device_id_type=MESH,
                ).start()

        orthogonalize(gathered, work, gram_ref, poly_ref, scatter)

    @pl.loop(0, MATS)
    def _(k):
        whole = ortho_out.at[k]
        pltpu.make_async_copy(whole, whole, srecv_sem.at[k]).wait()

        @pl.when(owner_of(k) != me)
        def _():
            pltpu.make_async_copy(nest.at[k], nest.at[k], gsend_sem.at[k]).wait()

    @pl.loop(0, CHUNKS)
    def _(c):
        for g in (0, 1):
            a_relay(g, c).wait_send()
            a_direct(g, c).wait_send()
            a_sum(g, c).wait_send()
            b_relay(g, c).wait_send()
            b_direct(g, c).wait_send()
            b_sum(g, c).wait_send()
        a_cross(c).wait_send()
        b_cross(c).wait_send()

    @pl.when(is_owner)
    def _():
        @pl.loop(0, COLS // NSW)
        def _(c):
            sent = work.at[pl.ds(0, SHARDS - 1), :, pl.ds(pl.multiple_of(c * NSW, NSW), NSW)]
            pltpu.make_async_copy(sent, sent, ssend_sem.at[c]).wait()


def body(grad_parts, momentum, weight):
    vmem = pl.BlockSpec(memory_space=pltpu.VMEM)
    grads = grad_parts.reshape(4, 2, MATS, BAND, COLS)
    a_block, b_block = (NA, BAND, COLS), (HB, BAND, COLS)

    def buf(*shape):
        return pltpu.VMEM(shape, BF16)

    moment, ortho = pl.pallas_call(
        kernel,
        out_shape=(
            jax.ShapeDtypeStruct((MATS, BAND, COLS), F32),
            jax.ShapeDtypeStruct((MATS, BAND, COLS), BF16),
        ),
        in_specs=[pl.BlockSpec(memory_space=pl.ANY), vmem],
        out_specs=(vmem, vmem),
        scratch_shapes=[
            buf(*a_block), buf(*a_block), buf(2, *a_block), buf(4, NB, BAND, COLS),
            buf(2, *a_block), buf(2, *a_block), buf(2, *a_block), buf(*a_block), buf(2, *a_block), buf(*a_block),
            buf(4, NB, BAND, COLS), buf(4, NB, BAND, COLS),
            buf(2, *b_block), buf(2, *b_block), buf(2, *b_block), buf(2, *b_block),
            buf(MATS, BAND, COLS),
            buf(SHARDS, BAND, COLS), buf(SHARDS, BAND, COLS),
            pltpu.VMEM((ROWS, ROWS), F32), pltpu.VMEM((ROWS, ROWS), BF16),
            pltpu.SemaphoreType.DMA((4,)),
            pltpu.SemaphoreType.DMA((KINDS, CHUNKS)), pltpu.SemaphoreType.DMA((KINDS, CHUNKS)),
            pltpu.SemaphoreType.DMA((MATS,)), pltpu.SemaphoreType.DMA((CHUNKS,)),
            pltpu.SemaphoreType.DMA((COLS // NSW,)), pltpu.SemaphoreType.DMA((MATS,)),
        ],
        compiler_params=pltpu.CompilerParams(
            collective_id=0, has_side_effects=True, vmem_limit_bytes=56 * 1024 * 1024
        ),
        name="muon_step",
    )(grads, momentum)
    shape_scale = 0.2 * math.sqrt(max(ROWS, COLS))
    scaled = shape_scale * ortho.astype(F32)
    fresh = (weight.astype(F32) - step_size * scaled).astype(BF16)
    return (moment, scaled, fresh)


def solution(mesh):
    return jax.shard_map(
        body,
        mesh=mesh,
        in_specs=(P("dp", None, "shard", None), P("dp", "shard", None), P("dp", "shard", None)),
        out_specs=(P("dp", "shard", None), P("dp", "shard", None), P("dp", "shard", None)),
        check_vma=False,
    )
```

```python
import functools
import math

import jax
import jax.numpy as jnp
from jax import lax
from jax.experimental import pallas as pl
from jax.experimental.pallas import tpu as pltpu
from jax.sharding import PartitionSpec as P

MESH = pl.DeviceIdType.MESH
F32 = jnp.float32
BF16 = jnp.bfloat16

MATS = 12
BATCHES = 2
MB = MATS // BATCHES
ROWS = 512
COLS = 2048
BAND = 16
SHARDS = 32
ITERS = 5
NA = 4
NB = MB - NA
HB = NB // 2

CHUNKS = 4
WIDTH = COLS // CHUNKS
STEPS = BATCHES * CHUNKS
AHEAD = 2
DONE = 1
EARLY = CHUNKS + 3
NSW = 2048
OUT = 512

linear_term = 3.4445
square_term = -4.775
fourth_term = 2.0315
decay_rate = 0.95
step_size = 0.05
tiny_norm = 1e-07

A_R, A_D, A_S, A_X, B_X, B_R, B_D, B_S = 0, 2, 4, 6, 7, 8, 10, 12
KINDS = 14


def owner_of(k):
    part, j = k // 6, k % 6
    side, i = j // 3, j % 3
    return side * 16 + ((8 * i + 4 * part) // 3) * 2


def owned(me):
    slot = -1
    for k in range(MATS):
        slot = jnp.where(me == owner_of(k), k, slot)
    return slot


def dot(a, b):
    return jnp.dot(a, b, preferred_element_type=F32)


def dot_t(a, b):
    return lax.dot_general(a, b, (((1,), (1,)), ((), ())), preferred_element_type=F32)


def poly_of(gram_ref, poly_ref, scale):
    half = ROWS // 2
    top = gram_ref[:half, :]
    low = gram_ref[half:, half:]
    high_top = top.astype(BF16)
    rest_top = (top - high_top.astype(F32)).astype(BF16)
    high_low = low.astype(BF16)
    rest_low = (low - high_low.astype(F32)).astype(BF16)
    corner = top[:, half:].T
    high_corner = corner.astype(BF16)
    rest_corner = (corner - high_corner.astype(F32)).astype(BF16)
    high_bottom = jnp.concatenate([high_corner, high_low], axis=1)
    rest_bottom = jnp.concatenate([rest_corner, rest_low], axis=1)
    high = jnp.concatenate([high_top, high_bottom], axis=0)
    rest = jnp.concatenate([rest_top, rest_bottom], axis=0)
    cross_top = dot(high_top, rest)
    cross_bottom = dot(high_bottom, rest)
    square_top = dot(high_top, high)
    square_low = dot(high_bottom, high[:, half:])
    flipped = jnp.concatenate([cross_top[:, :half].T, cross_bottom[:, :half].T], axis=1)
    poly_top = square_term * top + fourth_term * (square_top + (cross_top + flipped))
    cross_low = cross_bottom[:, half:]
    poly_low = square_term * low + fourth_term * (square_low + (cross_low + cross_low.T))
    poly_top = scale * poly_top
    poly_ref[:half, :] = poly_top.astype(BF16)
    poly_ref[half:, half:] = (scale * poly_low).astype(BF16)
    poly_ref[half:, :half] = poly_top[:, half:].T.astype(BF16)


def gram_of(block):
    half = ROWS // 2
    return dot_t(block[:half], block), dot_t(block[half:], block[half:])


def set_gram(gram_ref, block):
    half = ROWS // 2
    gram_ref[:half, :], gram_ref[half:, half:] = gram_of(block)


def add_gram(gram_ref, block):
    half = ROWS // 2
    top, low = gram_of(block)
    gram_ref[:half, :] += top
    gram_ref[half:, half:] += low


def begin(gram_ref, scale_ref):
    half = ROWS // 2
    row = lax.broadcasted_iota(jnp.int32, (half, half), 0)
    col = lax.broadcasted_iota(jnp.int32, (half, half), 1)
    diag = jnp.where(row == col, gram_ref[:half, :half] + gram_ref[half:, half:], 0.0)
    total = jnp.sum(jnp.sum(diag, axis=1, keepdims=True), axis=0, keepdims=True)
    scale = 1.0 / (jnp.sqrt(total) + tiny_norm)
    scale_ref[...] = jnp.broadcast_to(scale, scale_ref.shape)
    gram_ref[:half, :] *= scale * scale
    gram_ref[half:, half:] *= scale * scale


def poly_step(gram_ref, poly_ref, scale_ref):
    poly_of(gram_ref, poly_ref, scale_ref[:1, :1])


def apply_columns(matrix, poly_ref, scale_ref, cols, width):
    block = matrix[:, :, cols].reshape(ROWS, width)
    new = (linear_term * scale_ref[:1, :1]) * block.astype(F32) + dot(poly_ref[...], block)
    matrix[:, :, cols] = new.astype(BF16).reshape(SHARDS, BAND, width)


def apply_step(matrix, poly_ref, scale_ref):
    @pl.loop(0, COLS // NSW)
    def _(c):
        apply_columns(matrix, poly_ref, scale_ref, pl.ds(pl.multiple_of(c * NSW, NSW), NSW), NSW)


def gram_step(matrix, gram_ref, scale_ref):
    set_gram(gram_ref, matrix[...].reshape(ROWS, COLS))
    scale_ref[...] = jnp.ones_like(scale_ref)


def kernel(
    grads, momentum_hbm, moment_out, ortho_out,
    momentum,    own_p, own_m, own_c, own_b, a_r, a_d, a_s, a_x, a_send, ax_send,
    b_x, b_u, b_r, b_d, b_s, b_send,
    nest, gathered, gram_ref, poly_ref, scale_ref,
    load_sem, send_sem, recv_sem, gsend_sem, grecv_sem, ssend_sem, srecv_sem, greet_sem,
):
    dp = lax.axis_index("dp")
    me = lax.axis_index("shard")
    y, x = dp // 2, dp % 2
    other = 1 - x
    up_y, down_y, far_y = (y + 1) % 4, (y + 3) % 4, (y + 2) % 4
    up = (up_y * 2 + x, me)
    down = (down_y * 2 + x, me)
    partner = (y * 2 + other, me)
    way = (up, down)
    my_slot = owned(me)
    my_batch = jnp.where(my_slot >= 0, my_slot // MB, -1)

    loads = [
        pltpu.make_async_copy(grads.at[up_y, 0, :, pl.ds(0, NA)], own_p, load_sem.at[0]),
        pltpu.make_async_copy(grads.at[down_y, 1, :, pl.ds(0, NA)], own_m, load_sem.at[1]),
        pltpu.make_async_copy(grads.at[y, :, :, pl.ds(0, NA)], own_c, load_sem.at[2]),
        pltpu.make_async_copy(grads.at[:, x, :, pl.ds(NA, NB)], own_b, load_sem.at[3]),
        pltpu.make_async_copy(momentum_hbm, momentum, load_sem.at[4]),
    ]
    for load in loads:
        load.start()

    side, z, core = me // 16, (me // 2) % 8, me % 2

    def along_z(d):
        return (dp, side * 16 + ((z + d + 8) % 8) * 2 + core)

    def signal(semaphore, device):
        pl.semaphore_signal(semaphore, inc=1, device_id=device, device_id_type=MESH)

    barrier = pltpu.get_barrier_semaphore()
    greeted = [up, down, partner, along_z(1), along_z(-1)]
    greeted += [(dp, (1 - side) * 16 + z * 2 + core), (dp, me + 1 - 2 * core), (dp, (1 - side) * 16 + z * 2 + 1 - core)]
    for device in greeted:
        signal(barrier, device)
    pl.semaphore_wait(barrier, len(greeted))

    def greet(turn):
        if turn == 0:
            for d in (1, -1):
                signal(greet_sem.at[0], along_z(d))
        elif turn == 1:
            pl.semaphore_wait(greet_sem.at[0], 2)
            for d in (2, -2):
                signal(greet_sem.at[1], along_z(d))
        elif turn == 2:
            pl.semaphore_wait(greet_sem.at[1], 2)
            signal(greet_sem.at[2], along_z(4))
        else:
            pl.semaphore_wait(greet_sem.at[2], 1)

    greet(0)
    def columns(q):
        return pl.ds(pl.multiple_of((q % CHUNKS) * WIDTH, WIDTH), WIDTH)

    def message(kind, q, src, dst, device):
        return pltpu.make_async_remote_copy(
            src_ref=src, dst_ref=dst, send_sem=send_sem.at[kind], recv_sem=recv_sem.at[kind, q],
            device_id=device, device_id_type=MESH,
        )

    def a_relay(g, q):
        b, cols = q // CHUNKS, columns(q)
        return message(A_R + g, q, grads.at[far_y, g, b, pl.ds(0, NA), :, cols], a_r.at[g, b, :, :, cols], way[g])

    def a_direct(g, q):
        b, cols = q // CHUNKS, columns(q)
        target = (down_y, up_y)[g]
        return message(
            A_D + g, q, grads.at[target, g, b, pl.ds(0, NA), :, cols], a_d.at[g, b, :, :, cols], way[1 - g]
        )

    def a_sum(g, q):
        b, cols = q // CHUNKS, columns(q)
        return message(A_S + g, q, a_send.at[g, b, :, :, cols], a_s.at[g, b, :, :, cols], way[g])

    def a_cross(q):
        b, cols = q // CHUNKS, columns(q)
        return message(A_X, q, ax_send.at[b, :, :, cols], a_x.at[b, :, :, cols], partner)

    def b_cross(q):
        b, cols = q // CHUNKS, columns(q)
        return message(
            B_X, q, grads.at[:, other, b, pl.ds(NA, NB), :, cols], b_x.at[:, b, :, :, cols], partner
        )

    def b_relay(g, q):
        b, cols = q // CHUNKS, columns(q)
        return message(
            B_R + g, q, b_u.at[far_y, b, pl.ds(g * HB, HB), :, cols], b_r.at[g, b, :, :, cols], way[g]
        )

    def b_direct(g, q):
        b, cols = q // CHUNKS, columns(q)
        target = (down_y, up_y)[g]
        return message(
            B_D + g, q, b_u.at[target, b, pl.ds(g * HB, HB), :, cols], b_d.at[g, b, :, :, cols], way[1 - g]
        )

    def b_sum(g, q):
        b, cols = q // CHUNKS, columns(q)
        return message(B_S + g, q, b_send.at[g, b, :, :, cols], b_s.at[g, b, :, :, cols], way[g])

    def issue(q):
        b_cross(q).start()
        for g in (0, 1):
            a_relay(g, q).start()
        for g in (0, 1):
            a_direct(g, q).start()

    def stage1(q):
        b, cols = q // CHUNKS, columns(q)
        own = (own_p, own_m)
        for g in (0, 1):
            a_relay(g, q).wait_recv()
            total = own[g][b, :, :, cols].astype(F32) + a_r[g, b, :, :, cols].astype(F32)
            a_send[g, b, :, :, cols] = total.astype(BF16)
            a_sum(g, q).start()
        b_cross(q).wait_recv()
        for t in range(4):
            total = own_b[t, b, :, :, cols].astype(F32) + b_x[t, b, :, :, cols].astype(F32)
            b_u[t, b, :, :, cols] = total.astype(BF16)
        for g in (0, 1):
            b_relay(g, q).start()
        for g in (0, 1):
            b_direct(g, q).start()

    def a_total(g, q):
        b, cols = q // CHUNKS, columns(q)
        mine = own_c[g, b, :, :, cols].astype(F32)
        return mine + a_d[g, b, :, :, cols].astype(F32) + a_s[g, b, :, :, cols].astype(F32)

    def stage2(q):
        b, cols = q // CHUNKS, columns(q)
        for g in (0, 1):
            a_direct(g, q).wait_recv()
            a_sum(g, q).wait_recv()
        ax_send[b, :, :, cols] = a_total(other, q).astype(BF16)
        a_cross(q).start()
        own = (up_y, down_y)
        for g in (0, 1):
            b_relay(g, q).wait_recv()
            mine = own_b[own[g], b, g * HB:(g + 1) * HB, :, cols].astype(F32)
            crossed = b_x[own[g], b, g * HB:(g + 1) * HB, :, cols].astype(F32)
            b_send[g, b, :, :, cols] = (mine + crossed + b_r[g, b, :, :, cols].astype(F32)).astype(BF16)
            b_sum(g, q).start()

    def finish(b, first, gradient, cols):
        count = gradient.shape[0]
        moment = decay_rate * momentum[b, first:first + count, :, cols] + gradient
        moment_out[b, first:first + count, :, cols] = moment
        nest[b, first:first + count, :, cols] = (gradient + decay_rate * moment).astype(BF16)

    def stage3(q):
        b, cols = q // CHUNKS, columns(q)
        for g in (0, 1):
            b_direct(g, q).wait_recv()
            b_sum(g, q).wait_recv()
            mine = own_b[y, b, g * HB:(g + 1) * HB, :, cols].astype(F32)
            crossed = b_x[y, b, g * HB:(g + 1) * HB, :, cols].astype(F32)
            arrived = b_d[g, b, :, :, cols].astype(F32) + b_s[g, b, :, :, cols].astype(F32)
            finish(b, NA + g * HB, mine + crossed + arrived, cols)
        a_cross(q).wait_recv()
        finish(b, 0, a_total(x, q) + a_x[b, :, :, cols].astype(F32), cols)

        @pl.loop(0, MB)
        def _(j):
            owner = owner_of(b * MB + j)

            @pl.when(owner == me)
            def _():
                pltpu.make_async_copy(nest.at[b, j, :, cols], gathered.at[me, :, cols], grecv_sem.at[q]).start()

            @pl.when(owner != me)
            def _():
                pltpu.make_async_remote_copy(
                    src_ref=nest.at[b, j, :, cols], dst_ref=gathered.at[me, :, cols],
                    send_sem=gsend_sem.at[b, j], recv_sem=grecv_sem.at[q],
                    device_id=(dp, owner), device_id_type=MESH,
                ).start()

    def arrived(q):
        whole = gathered.at[:, :, columns(q)]
        pltpu.make_async_copy(whole, whole, grecv_sem.at[q]).wait()

    for q in range(AHEAD):
        issue(q)
    gram_ref[...] = jnp.zeros_like(gram_ref)
    for load in loads:
        load.wait()

    def guarded(step, offset, stage):
        @pl.when(jnp.logical_and(step >= offset, step < STEPS + offset))
        def _():
            stage(step - offset)

    @pl.loop(0, STEPS + 2)
    def _(step):
        turn = jnp.logical_and(my_batch == 0, jnp.logical_and(step >= EARLY, step < EARLY + DONE))

        @pl.when(jnp.logical_and(my_batch == 0, step == EARLY))
        def _():
            for q in range(CHUNKS):
                arrived(q)
            set_gram(gram_ref, gathered[...].reshape(ROWS, COLS))
            begin(gram_ref, scale_ref)

        guarded(step, 0, stage1)

        @pl.when(turn)
        def _():
            poly_step(gram_ref, poly_ref, scale_ref)

        for round in (0, 1, 2):
            pl.when(step == round)(functools.partial(greet, round + 1))
        guarded(step, 1, stage2)

        @pl.when(turn)
        def _():
            apply_step(gathered, poly_ref, scale_ref)

        guarded(step, 2, stage3)
        guarded(step, -AHEAD, issue)

        @pl.when(turn)
        def _():
            gram_step(gathered, gram_ref, scale_ref)

    @pl.when(my_batch == 1)
    def _():
        @pl.loop(CHUNKS, STEPS)
        def _(q):
            arrived(q)
            add_gram(gram_ref, gathered[:, :, columns(q)].reshape(ROWS, WIDTH))

        begin(gram_ref, scale_ref)

    @pl.when(my_batch >= 0)
    def _():
        @pl.loop(jnp.where(my_batch == 0, DONE, 0), ITERS - 1)
        def _(it):
            poly_step(gram_ref, poly_ref, scale_ref)
            apply_step(gathered, poly_ref, scale_ref)
            gram_step(gathered, gram_ref, scale_ref)

        poly_step(gram_ref, poly_ref, scale_ref)
        slot_batch, slot_j = my_slot // MB, my_slot % MB

        @pl.loop(0, COLS // OUT)
        def _(c):
            cols = pl.ds(pl.multiple_of(c * OUT, OUT), OUT)
            apply_columns(gathered, poly_ref, scale_ref, cols, OUT)
            target = ortho_out.at[slot_batch, slot_j, :, cols]
            pltpu.make_async_copy(gathered.at[me, :, cols], target, srecv_sem.at[slot_batch, slot_j]).start()

            @pl.loop(1, SHARDS)
            def _(r):
                to = (me + r) % SHARDS
                pltpu.make_async_remote_copy(
                    src_ref=gathered.at[to, :, cols], dst_ref=target,
                    send_sem=ssend_sem.at[c], recv_sem=srecv_sem.at[slot_batch, slot_j],
                    device_id=(dp, to), device_id_type=MESH,
                ).start()

    @pl.loop(0, MATS)
    def _(k):
        b, j = k // MB, k % MB

        @pl.when(owner_of(k) != me)
        def _():
            pltpu.make_async_copy(nest.at[b, j], nest.at[b, j], gsend_sem.at[b, j]).wait()

    def drain(kind, whole):
        pltpu.make_async_copy(whole, whole, send_sem.at[kind]).wait()

    for g in (0, 1):
        for kind in (A_R, A_D, A_S):
            drain(kind + g, a_s.at[g])
        for kind in (B_R, B_D, B_S):
            drain(kind + g, b_s.at[g])
    drain(A_X, a_x)
    drain(B_X, b_x)

    @pl.when(my_batch >= 0)
    def _():
        @pl.loop(0, COLS // OUT)
        def _(c):
            sent = gathered.at[pl.ds(0, SHARDS - 1), :, pl.ds(pl.multiple_of(c * OUT, OUT), OUT)]
            pltpu.make_async_copy(sent, sent, ssend_sem.at[c]).wait()

    @pl.loop(0, MATS)
    def _(k):
        whole = ortho_out.at[k // MB, k % MB]
        pltpu.make_async_copy(whole, whole, srecv_sem.at[k // MB, k % MB]).wait()


def body(grad_parts, momentum, weight):
    vmem = pl.BlockSpec(memory_space=pltpu.VMEM)
    grads = grad_parts.reshape(4, 2, BATCHES, MB, BAND, COLS)
    a_block, b_block = (BATCHES, NA, BAND, COLS), (BATCHES, HB, BAND, COLS)
    x_block = (BATCHES, NB, BAND, COLS)

    def buf(*shape):
        return pltpu.VMEM(shape, BF16)

    moment, ortho = pl.pallas_call(
        kernel,
        out_shape=(
            jax.ShapeDtypeStruct((BATCHES, MB, BAND, COLS), F32),
            jax.ShapeDtypeStruct((BATCHES, MB, BAND, COLS), BF16),
        ),
        in_specs=[pl.BlockSpec(memory_space=pl.ANY)] * 2,
        out_specs=(vmem, vmem),
        scratch_shapes=[
            pltpu.VMEM((BATCHES, MB, BAND, COLS), F32),
            buf(*a_block), buf(*a_block), buf(2, *a_block), buf(4, *x_block),
            buf(2, *a_block), buf(2, *a_block), buf(2, *a_block), buf(*a_block), buf(2, *a_block), buf(*a_block),
            buf(4, *x_block), buf(4, *x_block),
            buf(2, *b_block), buf(2, *b_block), buf(2, *b_block), buf(2, *b_block),
            buf(BATCHES, MB, BAND, COLS),
            buf(SHARDS, BAND, COLS),
            pltpu.VMEM((ROWS, ROWS), F32), pltpu.VMEM((ROWS, ROWS), BF16), pltpu.VMEM((8, 128), F32),
            pltpu.SemaphoreType.DMA((5,)),
            pltpu.SemaphoreType.DMA((KINDS,)), pltpu.SemaphoreType.DMA((KINDS, STEPS)),
            pltpu.SemaphoreType.DMA((BATCHES, MB)), pltpu.SemaphoreType.DMA((STEPS,)),
            pltpu.SemaphoreType.DMA((COLS // OUT,)), pltpu.SemaphoreType.DMA((BATCHES, MB)),
            pltpu.SemaphoreType.REGULAR((3,)),
        ],
        compiler_params=pltpu.CompilerParams(
            collective_id=0, has_side_effects=True, vmem_limit_bytes=56 * 1024 * 1024
        ),
        name="muon_step",
    )(grads, momentum.reshape(BATCHES, MB, BAND, COLS))
    shape_scale = 0.2 * math.sqrt(max(ROWS, COLS))
    scaled = shape_scale * ortho.reshape(MATS, BAND, COLS).astype(F32)
    fresh = (weight.astype(F32) - step_size * scaled).astype(BF16)
    return (moment.reshape(MATS, BAND, COLS), scaled, fresh)


def solution(mesh):
    return jax.shard_map(
        body,
        mesh=mesh,
        in_specs=(P("dp", None, "shard", None), P("dp", "shard", None), P("dp", "shard", None)),
        out_specs=(P("dp", "shard", None), P("dp", "shard", None), P("dp", "shard", None)),
        check_vma=False,
    )
```

```python
import functools
import math

import jax
import jax.numpy as jnp
from jax import lax
from jax.experimental import pallas as pl
from jax.experimental.pallas import tpu as pltpu
from jax.sharding import PartitionSpec as P

MESH = pl.DeviceIdType.MESH
F32 = jnp.float32
BF16 = jnp.bfloat16

MATS = 12
BATCHES = 2
MB = MATS // BATCHES
ROWS = 512
COLS = 2048
BAND = 16
SHARDS = 32
ITERS = 5
NA = 4
NB = MB - NA
HB = NB // 2

CHUNKS = 4
WIDTH = COLS // CHUNKS
STEPS = BATCHES * CHUNKS
AHEAD = 2
DONE = 1
EARLY = CHUNKS + 3
NSW = 2048
OUT = 1024

linear_term = 3.4445
square_term = -4.775
fourth_term = 2.0315
decay_rate = 0.95
step_size = 0.05
tiny_norm = 1e-07

A_R, A_D, A_S, A_X, B_X, B_R, B_D, B_S = 0, 2, 4, 6, 7, 8, 10, 12
KINDS = 14


def owner_of(k):
    part, j = k // 6, k % 6
    side, i = j // 3, j % 3
    return side * 16 + ((8 * i + 4 * part) // 3) * 2


def owned(me):
    slot = -1
    for k in range(MATS):
        slot = jnp.where(me == owner_of(k), k, slot)
    return slot


def dot(a, b):
    return jnp.dot(a, b, preferred_element_type=F32)


def dot_t(a, b):
    return lax.dot_general(a, b, (((1,), (1,)), ((), ())), preferred_element_type=F32)


def poly_of(gram_ref, poly_ref, scale):
    half = ROWS // 2
    top = gram_ref[:half, :]
    low = gram_ref[half:, half:]
    high_top = top.astype(BF16)
    rest_top = (top - high_top.astype(F32)).astype(BF16)
    high_low = low.astype(BF16)
    rest_low = (low - high_low.astype(F32)).astype(BF16)
    corner = top[:, half:].T
    high_corner = corner.astype(BF16)
    rest_corner = (corner - high_corner.astype(F32)).astype(BF16)
    high_bottom = jnp.concatenate([high_corner, high_low], axis=1)
    rest_bottom = jnp.concatenate([rest_corner, rest_low], axis=1)
    high = jnp.concatenate([high_top, high_bottom], axis=0)
    rest = jnp.concatenate([rest_top, rest_bottom], axis=0)
    cross_top = dot(high_top, rest)
    cross_bottom = dot(high_bottom, rest)
    square_top = dot(high_top, high)
    square_low = dot(high_bottom, high[:, half:])
    flipped = jnp.concatenate([cross_top[:, :half].T, cross_bottom[:, :half].T], axis=1)
    poly_top = square_term * top + fourth_term * (square_top + (cross_top + flipped))
    cross_low = cross_bottom[:, half:]
    poly_low = square_term * low + fourth_term * (square_low + (cross_low + cross_low.T))
    poly_top = scale * poly_top
    poly_ref[:half, :] = poly_top.astype(BF16)
    poly_ref[half:, half:] = (scale * poly_low).astype(BF16)
    poly_ref[half:, :half] = poly_top[:, half:].T.astype(BF16)


def gram_of(block):
    half = ROWS // 2
    return dot_t(block[:half], block), dot_t(block[half:], block[half:])


def set_gram(gram_ref, block):
    half = ROWS // 2
    gram_ref[:half, :], gram_ref[half:, half:] = gram_of(block)


def add_gram(gram_ref, block):
    half = ROWS // 2
    top, low = gram_of(block)
    gram_ref[:half, :] += top
    gram_ref[half:, half:] += low


def begin(gram_ref, scale_ref):
    half = ROWS // 2
    row = lax.broadcasted_iota(jnp.int32, (half, half), 0)
    col = lax.broadcasted_iota(jnp.int32, (half, half), 1)
    diag = jnp.where(row == col, gram_ref[:half, :half] + gram_ref[half:, half:], 0.0)
    total = jnp.sum(jnp.sum(diag, axis=1, keepdims=True), axis=0, keepdims=True)
    scale = 1.0 / (jnp.sqrt(total) + tiny_norm)
    scale_ref[...] = jnp.broadcast_to(scale, scale_ref.shape)
    gram_ref[:half, :] *= scale * scale
    gram_ref[half:, half:] *= scale * scale


def poly_step(gram_ref, poly_ref, scale_ref):
    poly_of(gram_ref, poly_ref, scale_ref[:1, :1])


def apply_columns(matrix, poly_ref, scale_ref, cols, width):
    block = matrix[:, :, cols].reshape(ROWS, width)
    new = (linear_term * scale_ref[:1, :1]) * block.astype(F32) + dot(poly_ref[...], block)
    matrix[:, :, cols] = new.astype(BF16).reshape(SHARDS, BAND, width)


def apply_step(matrix, poly_ref, scale_ref):
    @pl.loop(0, COLS // NSW)
    def _(c):
        apply_columns(matrix, poly_ref, scale_ref, pl.ds(pl.multiple_of(c * NSW, NSW), NSW), NSW)


def gram_step(matrix, gram_ref, scale_ref):
    set_gram(gram_ref, matrix[...].reshape(ROWS, COLS))
    scale_ref[...] = jnp.ones_like(scale_ref)


def kernel(
    grads, momentum_hbm, moment_hbm, ortho_out,
    momentum, moment_out,    own_p, own_m, own_c, own_b, a_r, a_d, a_s, a_x, a_send, ax_send,
    b_x, b_u, b_r, b_d, b_s, b_send,
    nest, gathered, gram_ref, poly_ref, scale_ref,
    load_sem, send_sem, recv_sem, gsend_sem, grecv_sem, ssend_sem, srecv_sem, greet_sem, moment_sem,
):
    dp = lax.axis_index("dp")
    me = lax.axis_index("shard")
    y, x = dp // 2, dp % 2
    other = 1 - x
    up_y, down_y, far_y = (y + 1) % 4, (y + 3) % 4, (y + 2) % 4
    up = (up_y * 2 + x, me)
    down = (down_y * 2 + x, me)
    partner = (y * 2 + other, me)
    way = (up, down)
    my_slot = owned(me)
    my_batch = jnp.where(my_slot >= 0, my_slot // MB, -1)

    loads = [
        pltpu.make_async_copy(grads.at[up_y, 0, :, pl.ds(0, NA)], own_p, load_sem.at[0]),
        pltpu.make_async_copy(grads.at[down_y, 1, :, pl.ds(0, NA)], own_m, load_sem.at[1]),
        pltpu.make_async_copy(grads.at[y, :, :, pl.ds(0, NA)], own_c, load_sem.at[2]),
        pltpu.make_async_copy(grads.at[:, x, :, pl.ds(NA, NB)], own_b, load_sem.at[3]),
        pltpu.make_async_copy(momentum_hbm, momentum, load_sem.at[4]),
    ]
    for load in loads:
        load.start()

    side, z, core = me // 16, (me // 2) % 8, me % 2

    def along_z(d):
        return (dp, side * 16 + ((z + d + 8) % 8) * 2 + core)

    def signal(semaphore, device):
        pl.semaphore_signal(semaphore, inc=1, device_id=device, device_id_type=MESH)

    barrier = pltpu.get_barrier_semaphore()
    greeted = [up, down, partner, along_z(1), along_z(-1)]
    greeted += [(dp, (1 - side) * 16 + z * 2 + core), (dp, me + 1 - 2 * core), (dp, (1 - side) * 16 + z * 2 + 1 - core)]
    for device in greeted:
        signal(barrier, device)
    pl.semaphore_wait(barrier, len(greeted))

    def greet(turn):
        if turn == 0:
            for d in (1, -1):
                signal(greet_sem.at[0], along_z(d))
        elif turn == 1:
            pl.semaphore_wait(greet_sem.at[0], 2)
            for d in (2, -2):
                signal(greet_sem.at[1], along_z(d))
        elif turn == 2:
            pl.semaphore_wait(greet_sem.at[1], 2)
            signal(greet_sem.at[2], along_z(4))
        else:
            pl.semaphore_wait(greet_sem.at[2], 1)

    greet(0)
    def columns(q):
        return pl.ds(pl.multiple_of((q % CHUNKS) * WIDTH, WIDTH), WIDTH)

    def message(kind, q, src, dst, device):
        return pltpu.make_async_remote_copy(
            src_ref=src, dst_ref=dst, send_sem=send_sem.at[kind], recv_sem=recv_sem.at[kind, q],
            device_id=device, device_id_type=MESH,
        )

    def a_relay(g, q):
        b, cols = q // CHUNKS, columns(q)
        return message(A_R + g, q, grads.at[far_y, g, b, pl.ds(0, NA), :, cols], a_r.at[g, b, :, :, cols], way[g])

    def a_direct(g, q):
        b, cols = q // CHUNKS, columns(q)
        target = (down_y, up_y)[g]
        return message(
            A_D + g, q, grads.at[target, g, b, pl.ds(0, NA), :, cols], a_d.at[g, b, :, :, cols], way[1 - g]
        )

    def a_sum(g, q):
        b, cols = q // CHUNKS, columns(q)
        return message(A_S + g, q, a_send.at[g, b, :, :, cols], a_s.at[g, b, :, :, cols], way[g])

    def a_cross(q):
        b, cols = q // CHUNKS, columns(q)
        return message(A_X, q, ax_send.at[b, :, :, cols], a_x.at[b, :, :, cols], partner)

    def b_cross(q):
        b, cols = q // CHUNKS, columns(q)
        return message(
            B_X, q, grads.at[:, other, b, pl.ds(NA, NB), :, cols], b_x.at[:, b, :, :, cols], partner
        )

    def b_relay(g, q):
        b, cols = q // CHUNKS, columns(q)
        return message(
            B_R + g, q, b_u.at[far_y, b, pl.ds(g * HB, HB), :, cols], b_r.at[g, b, :, :, cols], way[g]
        )

    def b_direct(g, q):
        b, cols = q // CHUNKS, columns(q)
        target = (down_y, up_y)[g]
        return message(
            B_D + g, q, b_u.at[target, b, pl.ds(g * HB, HB), :, cols], b_d.at[g, b, :, :, cols], way[1 - g]
        )

    def b_sum(g, q):
        b, cols = q // CHUNKS, columns(q)
        return message(B_S + g, q, b_send.at[g, b, :, :, cols], b_s.at[g, b, :, :, cols], way[g])

    def issue(q):
        b_cross(q).start()
        for g in (0, 1):
            a_relay(g, q).start()
        for g in (0, 1):
            a_direct(g, q).start()

    def stage1(q):
        b, cols = q // CHUNKS, columns(q)
        own = (own_p, own_m)
        for g in (0, 1):
            a_relay(g, q).wait_recv()
            total = own[g][b, :, :, cols].astype(F32) + a_r[g, b, :, :, cols].astype(F32)
            a_send[g, b, :, :, cols] = total.astype(BF16)
            a_sum(g, q).start()
        b_cross(q).wait_recv()
        for t in range(4):
            total = own_b[t, b, :, :, cols].astype(F32) + b_x[t, b, :, :, cols].astype(F32)
            b_u[t, b, :, :, cols] = total.astype(BF16)
        for g in (0, 1):
            b_relay(g, q).start()
        for g in (0, 1):
            b_direct(g, q).start()

    def a_total(g, q):
        b, cols = q // CHUNKS, columns(q)
        mine = own_c[g, b, :, :, cols].astype(F32)
        return mine + a_d[g, b, :, :, cols].astype(F32) + a_s[g, b, :, :, cols].astype(F32)

    def stage2(q):
        b, cols = q // CHUNKS, columns(q)
        for g in (0, 1):
            a_direct(g, q).wait_recv()
            a_sum(g, q).wait_recv()
        ax_send[b, :, :, cols] = a_total(other, q).astype(BF16)
        a_cross(q).start()
        own = (up_y, down_y)
        for g in (0, 1):
            b_relay(g, q).wait_recv()
            mine = own_b[own[g], b, g * HB:(g + 1) * HB, :, cols].astype(F32)
            crossed = b_x[own[g], b, g * HB:(g + 1) * HB, :, cols].astype(F32)
            b_send[g, b, :, :, cols] = (mine + crossed + b_r[g, b, :, :, cols].astype(F32)).astype(BF16)
            b_sum(g, q).start()

    def finish(b, first, gradient, cols):
        count = gradient.shape[0]
        moment = decay_rate * momentum[b, first:first + count, :, cols] + gradient
        moment_out[b, first:first + count, :, cols] = moment
        nest[b, first:first + count, :, cols] = (gradient + decay_rate * moment).astype(BF16)

    def moment_store(q):
        b, cols = q // CHUNKS, columns(q)
        return pltpu.make_async_copy(moment_out.at[b, :, :, cols], moment_hbm.at[b, :, :, cols], moment_sem.at[q])

    def stage3(q):
        b, cols = q // CHUNKS, columns(q)
        for g in (0, 1):
            b_direct(g, q).wait_recv()
            b_sum(g, q).wait_recv()
            mine = own_b[y, b, g * HB:(g + 1) * HB, :, cols].astype(F32)
            crossed = b_x[y, b, g * HB:(g + 1) * HB, :, cols].astype(F32)
            arrived = b_d[g, b, :, :, cols].astype(F32) + b_s[g, b, :, :, cols].astype(F32)
            finish(b, NA + g * HB, mine + crossed + arrived, cols)
        a_cross(q).wait_recv()
        finish(b, 0, a_total(x, q) + a_x[b, :, :, cols].astype(F32), cols)
        moment_store(q).start()

        @pl.loop(0, MB)
        def _(j):
            owner = owner_of(b * MB + j)

            @pl.when(owner == me)
            def _():
                pltpu.make_async_copy(nest.at[b, j, :, cols], gathered.at[me, :, cols], grecv_sem.at[q]).start()

            @pl.when(owner != me)
            def _():
                pltpu.make_async_remote_copy(
                    src_ref=nest.at[b, j, :, cols], dst_ref=gathered.at[me, :, cols],
                    send_sem=gsend_sem.at[b, j], recv_sem=grecv_sem.at[q],
                    device_id=(dp, owner), device_id_type=MESH,
                ).start()

    def arrived(q):
        whole = gathered.at[:, :, columns(q)]
        pltpu.make_async_copy(whole, whole, grecv_sem.at[q]).wait()

    for q in range(AHEAD):
        issue(q)
    gram_ref[...] = jnp.zeros_like(gram_ref)
    for load in loads:
        load.wait()

    def guarded(step, offset, stage):
        @pl.when(jnp.logical_and(step >= offset, step < STEPS + offset))
        def _():
            stage(step - offset)

    @pl.loop(0, STEPS + 2)
    def _(step):
        turn = jnp.logical_and(my_batch == 0, jnp.logical_and(step >= EARLY, step < EARLY + DONE))

        @pl.when(jnp.logical_and(my_batch == 0, step == EARLY))
        def _():
            for q in range(CHUNKS):
                arrived(q)
            set_gram(gram_ref, gathered[...].reshape(ROWS, COLS))
            begin(gram_ref, scale_ref)

        guarded(step, 0, stage1)

        @pl.when(turn)
        def _():
            poly_step(gram_ref, poly_ref, scale_ref)

        for round in (0, 1, 2):
            pl.when(step == round)(functools.partial(greet, round + 1))
        guarded(step, 1, stage2)

        @pl.when(turn)
        def _():
            apply_step(gathered, poly_ref, scale_ref)

        guarded(step, 2, stage3)
        guarded(step, -AHEAD, issue)

        @pl.when(turn)
        def _():
            gram_step(gathered, gram_ref, scale_ref)

    @pl.when(my_batch == 1)
    def _():
        @pl.loop(CHUNKS, STEPS)
        def _(q):
            arrived(q)
            add_gram(gram_ref, gathered[:, :, columns(q)].reshape(ROWS, WIDTH))

        begin(gram_ref, scale_ref)

    @pl.when(my_batch >= 0)
    def _():
        @pl.loop(jnp.where(my_batch == 0, DONE, 0), ITERS - 1)
        def _(it):
            poly_step(gram_ref, poly_ref, scale_ref)
            apply_step(gathered, poly_ref, scale_ref)
            gram_step(gathered, gram_ref, scale_ref)

        poly_step(gram_ref, poly_ref, scale_ref)
        slot_batch, slot_j = my_slot // MB, my_slot % MB

        @pl.loop(0, COLS // OUT)
        def _(c):
            cols = pl.ds(pl.multiple_of(c * OUT, OUT), OUT)
            apply_columns(gathered, poly_ref, scale_ref, cols, OUT)
            target = ortho_out.at[slot_batch, slot_j, :, cols]
            pltpu.make_async_copy(gathered.at[me, :, cols], target, srecv_sem.at[slot_batch, slot_j]).start()

            @pl.loop(1, SHARDS)
            def _(r):
                to = (me + r) % SHARDS
                pltpu.make_async_remote_copy(
                    src_ref=gathered.at[to, :, cols], dst_ref=target,
                    send_sem=ssend_sem.at[c], recv_sem=srecv_sem.at[slot_batch, slot_j],
                    device_id=(dp, to), device_id_type=MESH,
                ).start()

    @pl.loop(0, MATS)
    def _(k):
        b, j = k // MB, k % MB

        @pl.when(owner_of(k) != me)
        def _():
            pltpu.make_async_copy(nest.at[b, j], nest.at[b, j], gsend_sem.at[b, j]).wait()

    @pl.loop(0, STEPS)
    def _(q):
        moment_store(q).wait()

    def drain(kind, whole):
        pltpu.make_async_copy(whole, whole, send_sem.at[kind]).wait()

    for g in (0, 1):
        for kind in (A_R, A_D, A_S):
            drain(kind + g, a_s.at[g])
        for kind in (B_R, B_D, B_S):
            drain(kind + g, b_s.at[g])
    drain(A_X, a_x)
    drain(B_X, b_x)

    @pl.when(my_batch >= 0)
    def _():
        @pl.loop(0, COLS // OUT)
        def _(c):
            sent = gathered.at[pl.ds(0, SHARDS - 1), :, pl.ds(pl.multiple_of(c * OUT, OUT), OUT)]
            pltpu.make_async_copy(sent, sent, ssend_sem.at[c]).wait()

    @pl.loop(0, MATS)
    def _(k):
        whole = ortho_out.at[k // MB, k % MB]
        pltpu.make_async_copy(whole, whole, srecv_sem.at[k // MB, k % MB]).wait()


PIECE = 3


def outputs(moment, ortho, weight, moment_out, update_out, weight_out):
    moment_out[...] = moment[...]
    scaled = (0.2 * math.sqrt(max(ROWS, COLS))) * ortho[...].astype(F32)
    update_out[...] = scaled
    weight_out[...] = (weight[...].astype(F32) - step_size * scaled).astype(BF16)


def body(grad_parts, momentum, weight):
    grads = grad_parts.reshape(4, 2, BATCHES, MB, BAND, COLS)
    a_block, b_block = (BATCHES, NA, BAND, COLS), (BATCHES, HB, BAND, COLS)
    x_block = (BATCHES, NB, BAND, COLS)

    def buf(*shape):
        return pltpu.VMEM(shape, BF16)

    moment, ortho = pl.pallas_call(
        kernel,
        out_shape=(
            jax.ShapeDtypeStruct((BATCHES, MB, BAND, COLS), F32),
            jax.ShapeDtypeStruct((BATCHES, MB, BAND, COLS), BF16),
        ),
        in_specs=[pl.BlockSpec(memory_space=pl.ANY)] * 2,
        out_specs=(pl.BlockSpec(memory_space=pl.ANY),) * 2,
        scratch_shapes=[
            pltpu.VMEM((BATCHES, MB, BAND, COLS), F32), pltpu.VMEM((BATCHES, MB, BAND, COLS), F32),
            buf(*a_block), buf(*a_block), buf(2, *a_block), buf(4, *x_block),
            buf(2, *a_block), buf(2, *a_block), buf(2, *a_block), buf(*a_block), buf(2, *a_block), buf(*a_block),
            buf(4, *x_block), buf(4, *x_block),
            buf(2, *b_block), buf(2, *b_block), buf(2, *b_block), buf(2, *b_block),
            buf(BATCHES, MB, BAND, COLS),
            buf(SHARDS, BAND, COLS),
            pltpu.VMEM((ROWS, ROWS), F32), pltpu.VMEM((ROWS, ROWS), BF16), pltpu.VMEM((8, 128), F32),
            pltpu.SemaphoreType.DMA((5,)),
            pltpu.SemaphoreType.DMA((KINDS,)), pltpu.SemaphoreType.DMA((KINDS, STEPS)),
            pltpu.SemaphoreType.DMA((BATCHES, MB)), pltpu.SemaphoreType.DMA((STEPS,)),
            pltpu.SemaphoreType.DMA((COLS // OUT,)), pltpu.SemaphoreType.DMA((BATCHES, MB)),
            pltpu.SemaphoreType.REGULAR((3,)), pltpu.SemaphoreType.DMA((STEPS,)),
        ],
        compiler_params=pltpu.CompilerParams(
            collective_id=0, has_side_effects=True, vmem_limit_bytes=56 * 1024 * 1024
        ),
        name="muon_step",
    )(grads, momentum.reshape(BATCHES, MB, BAND, COLS))
    block = pl.BlockSpec((PIECE, BAND, COLS), lambda i: (i, 0, 0))
    return tuple(
        pl.pallas_call(
            outputs,
            grid=(MATS // PIECE,),
            out_shape=(
                jax.ShapeDtypeStruct((MATS, BAND, COLS), F32),
                jax.ShapeDtypeStruct((MATS, BAND, COLS), F32),
                jax.ShapeDtypeStruct((MATS, BAND, COLS), BF16),
            ),
            in_specs=[block] * 3,
            out_specs=(block,) * 3,
            compiler_params=pltpu.CompilerParams(vmem_limit_bytes=56 * 1024 * 1024),
            name="outputs",
        )(moment.reshape(MATS, BAND, COLS), ortho.reshape(MATS, BAND, COLS), weight)
    )


def solution(mesh):
    return jax.shard_map(
        body,
        mesh=mesh,
        in_specs=(P("dp", None, "shard", None), P("dp", "shard", None), P("dp", "shard", None)),
        out_specs=(P("dp", "shard", None), P("dp", "shard", None), P("dp", "shard", None)),
        check_vma=False,
    )
```

```python
import functools
import math

import jax
import jax.numpy as jnp
from jax import lax
from jax.experimental import pallas as pl
from jax.experimental.pallas import tpu as pltpu
from jax.sharding import PartitionSpec as P

MESH = pl.DeviceIdType.MESH
F32 = jnp.float32
BF16 = jnp.bfloat16

MATS = 12
BATCHES = 2
MB = MATS // BATCHES
ROWS = 512
COLS = 2048
BAND = 16
SHARDS = 32
ITERS = 5
NA = 4
NB = MB - NA
HB = NB // 2

CHUNKS = 4
WIDTH = COLS // CHUNKS
STEPS = BATCHES * CHUNKS
AHEAD = 2
DONE = 1
EARLY = CHUNKS + 3
NSW = 2048
OUT = 2048

linear_term = 3.4445
square_term = -4.775
fourth_term = 2.0315
decay_rate = 0.95
step_size = 0.05
tiny_norm = 1e-07

A_R, A_D, A_S, A_X, B_X, B_R, B_D, B_S = 0, 2, 4, 6, 7, 8, 10, 12
KINDS = 14


def owner_of(k):
    part, j = k // 6, k % 6
    side, i = j // 3, j % 3
    return side * 16 + ((8 * i + 4 * part) // 3) * 2


def owned(me):
    slot = -1
    for k in range(MATS):
        slot = jnp.where(me == owner_of(k), k, slot)
    return slot


def dot(a, b):
    return jnp.dot(a, b, preferred_element_type=F32)


def dot_t(a, b):
    return lax.dot_general(a, b, (((1,), (1,)), ((), ())), preferred_element_type=F32)


def poly_of(gram_ref, poly_ref, scale):
    half = ROWS // 2
    top = gram_ref[:half, :]
    low = gram_ref[half:, half:]
    high_top = top.astype(BF16)
    rest_top = (top - high_top.astype(F32)).astype(BF16)
    high_low = low.astype(BF16)
    rest_low = (low - high_low.astype(F32)).astype(BF16)
    corner = top[:, half:].T
    high_corner = corner.astype(BF16)
    rest_corner = (corner - high_corner.astype(F32)).astype(BF16)
    high_bottom = jnp.concatenate([high_corner, high_low], axis=1)
    rest_bottom = jnp.concatenate([rest_corner, rest_low], axis=1)
    high = jnp.concatenate([high_top, high_bottom], axis=0)
    rest = jnp.concatenate([rest_top, rest_bottom], axis=0)
    cross_top = dot(high_top, rest)
    cross_bottom = dot(high_bottom, rest)
    square_top = dot(high_top, high)
    square_low = dot(high_bottom, high[:, half:])
    flipped = jnp.concatenate([cross_top[:, :half].T, cross_bottom[:, :half].T], axis=1)
    poly_top = square_term * top + fourth_term * (square_top + (cross_top + flipped))
    cross_low = cross_bottom[:, half:]
    poly_low = square_term * low + fourth_term * (square_low + (cross_low + cross_low.T))
    poly_top = scale * poly_top
    poly_ref[:half, :] = poly_top.astype(BF16)
    poly_ref[half:, half:] = (scale * poly_low).astype(BF16)
    poly_ref[half:, :half] = poly_top[:, half:].T.astype(BF16)


def gram_of(block):
    half = ROWS // 2
    return dot_t(block[:half], block), dot_t(block[half:], block[half:])


def set_gram(gram_ref, block):
    half = ROWS // 2
    gram_ref[:half, :], gram_ref[half:, half:] = gram_of(block)


def add_gram(gram_ref, block):
    half = ROWS // 2
    top, low = gram_of(block)
    gram_ref[:half, :] += top
    gram_ref[half:, half:] += low


def begin(gram_ref, scale_ref):
    half = ROWS // 2
    row = lax.broadcasted_iota(jnp.int32, (half, half), 0)
    col = lax.broadcasted_iota(jnp.int32, (half, half), 1)
    diag = jnp.where(row == col, gram_ref[:half, :half] + gram_ref[half:, half:], 0.0)
    total = jnp.sum(jnp.sum(diag, axis=1, keepdims=True), axis=0, keepdims=True)
    scale = 1.0 / (jnp.sqrt(total) + tiny_norm)
    scale_ref[...] = jnp.broadcast_to(scale, scale_ref.shape)
    gram_ref[:half, :] *= scale * scale
    gram_ref[half:, half:] *= scale * scale


def poly_step(gram_ref, poly_ref, scale_ref):
    poly_of(gram_ref, poly_ref, scale_ref[:1, :1])


def apply_columns(matrix, poly_ref, scale_ref, cols, width):
    block = matrix[:, :, cols].reshape(ROWS, width)
    new = (linear_term * scale_ref[:1, :1]) * block.astype(F32) + dot(poly_ref[...], block)
    matrix[:, :, cols] = new.astype(BF16).reshape(SHARDS, BAND, width)


def apply_step(matrix, poly_ref, scale_ref):
    @pl.loop(0, COLS // NSW)
    def _(c):
        apply_columns(matrix, poly_ref, scale_ref, pl.ds(pl.multiple_of(c * NSW, NSW), NSW), NSW)


def gram_step(matrix, gram_ref, scale_ref):
    set_gram(gram_ref, matrix[...].reshape(ROWS, COLS))
    scale_ref[...] = jnp.ones_like(scale_ref)


def kernel(
    grads, momentum_hbm, moment_hbm, ortho_out,
    momentum, moment_out,    own_p, own_m, own_c, own_b, a_r, a_d, a_s, a_x, a_send, ax_send,
    b_x, b_u, b_r, b_d, b_s, b_send,
    nest, gathered, gram_ref, poly_ref, scale_ref,
    load_sem, send_sem, recv_sem, gsend_sem, grecv_sem, ssend_sem, srecv_sem, greet_sem, moment_sem,
):
    dp = lax.axis_index("dp")
    me = lax.axis_index("shard")
    y, x = dp // 2, dp % 2
    other = 1 - x
    up_y, down_y, far_y = (y + 1) % 4, (y + 3) % 4, (y + 2) % 4
    up = (up_y * 2 + x, me)
    down = (down_y * 2 + x, me)
    partner = (y * 2 + other, me)
    way = (up, down)
    my_slot = owned(me)
    my_batch = jnp.where(my_slot >= 0, my_slot // MB, -1)

    loads = [
        pltpu.make_async_copy(grads.at[up_y, 0, :, pl.ds(0, NA)], own_p, load_sem.at[0]),
        pltpu.make_async_copy(grads.at[down_y, 1, :, pl.ds(0, NA)], own_m, load_sem.at[1]),
        pltpu.make_async_copy(grads.at[y, :, :, pl.ds(0, NA)], own_c, load_sem.at[2]),
        pltpu.make_async_copy(grads.at[:, x, :, pl.ds(NA, NB)], own_b, load_sem.at[3]),
        pltpu.make_async_copy(momentum_hbm, momentum, load_sem.at[4]),
    ]
    for load in loads:
        load.start()

    side, z, core = me // 16, (me // 2) % 8, me % 2

    def along_z(d):
        return (dp, side * 16 + ((z + d + 8) % 8) * 2 + core)

    def signal(semaphore, device):
        pl.semaphore_signal(semaphore, inc=1, device_id=device, device_id_type=MESH)

    barrier = pltpu.get_barrier_semaphore()
    greeted = [up, down, partner, along_z(1), along_z(-1)]
    greeted += [(dp, (1 - side) * 16 + z * 2 + core), (dp, me + 1 - 2 * core), (dp, (1 - side) * 16 + z * 2 + 1 - core)]
    for device in greeted:
        signal(barrier, device)
    pl.semaphore_wait(barrier, len(greeted))

    def greet(turn):
        if turn == 0:
            for d in (1, -1):
                signal(greet_sem.at[0], along_z(d))
        elif turn == 1:
            pl.semaphore_wait(greet_sem.at[0], 2)
            for d in (2, -2):
                signal(greet_sem.at[1], along_z(d))
        elif turn == 2:
            pl.semaphore_wait(greet_sem.at[1], 2)
            signal(greet_sem.at[2], along_z(4))
        else:
            pl.semaphore_wait(greet_sem.at[2], 1)

    greet(0)
    def columns(q):
        return pl.ds(pl.multiple_of((q % CHUNKS) * WIDTH, WIDTH), WIDTH)

    def message(kind, q, src, dst, device):
        return pltpu.make_async_remote_copy(
            src_ref=src, dst_ref=dst, send_sem=send_sem.at[kind], recv_sem=recv_sem.at[kind, q],
            device_id=device, device_id_type=MESH,
        )

    def a_relay(g, q):
        b, cols = q // CHUNKS, columns(q)
        return message(A_R + g, q, grads.at[far_y, g, b, pl.ds(0, NA), :, cols], a_r.at[g, b, :, :, cols], way[g])

    def a_direct(g, q):
        b, cols = q // CHUNKS, columns(q)
        target = (down_y, up_y)[g]
        return message(
            A_D + g, q, grads.at[target, g, b, pl.ds(0, NA), :, cols], a_d.at[g, b, :, :, cols], way[1 - g]
        )

    def a_sum(g, q):
        b, cols = q // CHUNKS, columns(q)
        return message(A_S + g, q, a_send.at[g, b, :, :, cols], a_s.at[g, b, :, :, cols], way[g])

    def a_cross(q):
        b, cols = q // CHUNKS, columns(q)
        return message(A_X, q, ax_send.at[b, :, :, cols], a_x.at[b, :, :, cols], partner)

    def b_cross(q):
        b, cols = q // CHUNKS, columns(q)
        return message(
            B_X, q, grads.at[:, other, b, pl.ds(NA, NB), :, cols], b_x.at[:, b, :, :, cols], partner
        )

    def b_relay(g, q):
        b, cols = q // CHUNKS, columns(q)
        return message(
            B_R + g, q, b_u.at[far_y, b, pl.ds(g * HB, HB), :, cols], b_r.at[g, b, :, :, cols], way[g]
        )

    def b_direct(g, q):
        b, cols = q // CHUNKS, columns(q)
        target = (down_y, up_y)[g]
        return message(
            B_D + g, q, b_u.at[target, b, pl.ds(g * HB, HB), :, cols], b_d.at[g, b, :, :, cols], way[1 - g]
        )

    def b_sum(g, q):
        b, cols = q // CHUNKS, columns(q)
        return message(B_S + g, q, b_send.at[g, b, :, :, cols], b_s.at[g, b, :, :, cols], way[g])

    def issue(q):
        b_cross(q).start()
        for g in (0, 1):
            a_relay(g, q).start()
        for g in (0, 1):
            a_direct(g, q).start()

    def stage1(q):
        b, cols = q // CHUNKS, columns(q)
        own = (own_p, own_m)
        for g in (0, 1):
            a_relay(g, q).wait_recv()
            total = own[g][b, :, :, cols].astype(F32) + a_r[g, b, :, :, cols].astype(F32)
            a_send[g, b, :, :, cols] = total.astype(BF16)
            a_sum(g, q).start()
        b_cross(q).wait_recv()
        for t in range(4):
            total = own_b[t, b, :, :, cols].astype(F32) + b_x[t, b, :, :, cols].astype(F32)
            b_u[t, b, :, :, cols] = total.astype(BF16)
        for g in (0, 1):
            b_relay(g, q).start()
        for g in (0, 1):
            b_direct(g, q).start()

    def a_total(g, q):
        b, cols = q // CHUNKS, columns(q)
        mine = own_c[g, b, :, :, cols].astype(F32)
        return mine + a_d[g, b, :, :, cols].astype(F32) + a_s[g, b, :, :, cols].astype(F32)

    def stage2(q):
        b, cols = q // CHUNKS, columns(q)
        for g in (0, 1):
            a_direct(g, q).wait_recv()
            a_sum(g, q).wait_recv()
        ax_send[b, :, :, cols] = a_total(other, q).astype(BF16)
        a_cross(q).start()
        own = (up_y, down_y)
        for g in (0, 1):
            b_relay(g, q).wait_recv()
            mine = own_b[own[g], b, g * HB:(g + 1) * HB, :, cols].astype(F32)
            crossed = b_x[own[g], b, g * HB:(g + 1) * HB, :, cols].astype(F32)
            b_send[g, b, :, :, cols] = (mine + crossed + b_r[g, b, :, :, cols].astype(F32)).astype(BF16)
            b_sum(g, q).start()

    def finish(b, first, gradient, cols):
        count = gradient.shape[0]
        moment = decay_rate * momentum[b, first:first + count, :, cols] + gradient
        moment_out[b, first:first + count, :, cols] = moment
        nest[b, first:first + count, :, cols] = (gradient + decay_rate * moment).astype(BF16)

    def moment_store(q):
        b, cols = q // CHUNKS, columns(q)
        return pltpu.make_async_copy(moment_out.at[b, :, :, cols], moment_hbm.at[b, :, :, cols], moment_sem.at[q])

    def to_owners(q, first, last):
        b, cols = q // CHUNKS, columns(q)

        @pl.loop(first, last)
        def _(j):
            owner = owner_of(b * MB + j)

            @pl.when(owner == me)
            def _():
                pltpu.make_async_copy(nest.at[b, j, :, cols], gathered.at[me, :, cols], grecv_sem.at[q]).start()

            @pl.when(owner != me)
            def _():
                pltpu.make_async_remote_copy(
                    src_ref=nest.at[b, j, :, cols], dst_ref=gathered.at[me, :, cols],
                    send_sem=gsend_sem.at[b, j], recv_sem=grecv_sem.at[q],
                    device_id=(dp, owner), device_id_type=MESH,
                ).start()

    def stage3(q):
        b, cols = q // CHUNKS, columns(q)
        for g in (0, 1):
            b_direct(g, q).wait_recv()
            b_sum(g, q).wait_recv()
            mine = own_b[y, b, g * HB:(g + 1) * HB, :, cols].astype(F32)
            crossed = b_x[y, b, g * HB:(g + 1) * HB, :, cols].astype(F32)
            arrived = b_d[g, b, :, :, cols].astype(F32) + b_s[g, b, :, :, cols].astype(F32)
            finish(b, NA + g * HB, mine + crossed + arrived, cols)
        to_owners(q, NA, MB)
        a_cross(q).wait_recv()
        finish(b, 0, a_total(x, q) + a_x[b, :, :, cols].astype(F32), cols)
        moment_store(q).start()

        to_owners(q, 0, NA)

    def arrived(q):
        whole = gathered.at[:, :, columns(q)]
        pltpu.make_async_copy(whole, whole, grecv_sem.at[q]).wait()

    for q in range(AHEAD):
        issue(q)
    gram_ref[...] = jnp.zeros_like(gram_ref)
    for load in loads:
        load.wait()

    def guarded(step, offset, stage):
        @pl.when(jnp.logical_and(step >= offset, step < STEPS + offset))
        def _():
            stage(step - offset)

    @pl.loop(0, STEPS + 2)
    def _(step):
        turn = jnp.logical_and(my_batch == 0, jnp.logical_and(step >= EARLY, step < EARLY + DONE))

        @pl.when(jnp.logical_and(my_batch == 0, step == EARLY))
        def _():
            for q in range(CHUNKS):
                arrived(q)
            set_gram(gram_ref, gathered[...].reshape(ROWS, COLS))
            begin(gram_ref, scale_ref)

        guarded(step, 0, stage1)

        @pl.when(turn)
        def _():
            poly_step(gram_ref, poly_ref, scale_ref)

        for round in (0, 1, 2):
            pl.when(step == round)(functools.partial(greet, round + 1))
        guarded(step, 1, stage2)

        @pl.when(turn)
        def _():
            apply_step(gathered, poly_ref, scale_ref)

        guarded(step, 2, stage3)
        guarded(step, -AHEAD, issue)

        @pl.when(turn)
        def _():
            gram_step(gathered, gram_ref, scale_ref)

    @pl.when(my_batch == 1)
    def _():
        @pl.loop(CHUNKS, STEPS)
        def _(q):
            arrived(q)
            add_gram(gram_ref, gathered[:, :, columns(q)].reshape(ROWS, WIDTH))

        begin(gram_ref, scale_ref)

    @pl.when(my_batch >= 0)
    def _():
        @pl.loop(jnp.where(my_batch == 0, DONE, 0), ITERS - 1)
        def _(it):
            poly_step(gram_ref, poly_ref, scale_ref)
            apply_step(gathered, poly_ref, scale_ref)
            gram_step(gathered, gram_ref, scale_ref)

        poly_step(gram_ref, poly_ref, scale_ref)
        slot_batch, slot_j = my_slot // MB, my_slot % MB

        @pl.loop(0, COLS // OUT)
        def _(c):
            cols = pl.ds(pl.multiple_of(c * OUT, OUT), OUT)
            apply_columns(gathered, poly_ref, scale_ref, cols, OUT)
            target = ortho_out.at[slot_batch, slot_j, :, cols]
            pltpu.make_async_copy(gathered.at[me, :, cols], target, srecv_sem.at[slot_batch, slot_j]).start()

            @pl.loop(1, SHARDS)
            def _(r):
                to = (me + r) % SHARDS
                pltpu.make_async_remote_copy(
                    src_ref=gathered.at[to, :, cols], dst_ref=target,
                    send_sem=ssend_sem.at[c], recv_sem=srecv_sem.at[slot_batch, slot_j],
                    device_id=(dp, to), device_id_type=MESH,
                ).start()

    @pl.loop(0, MATS)
    def _(k):
        b, j = k // MB, k % MB

        @pl.when(owner_of(k) != me)
        def _():
            pltpu.make_async_copy(nest.at[b, j], nest.at[b, j], gsend_sem.at[b, j]).wait()

    @pl.loop(0, STEPS)
    def _(q):
        moment_store(q).wait()

    def drain(kind, whole):
        pltpu.make_async_copy(whole, whole, send_sem.at[kind]).wait()

    for g in (0, 1):
        for kind in (A_R, A_D, A_S):
            drain(kind + g, a_s.at[g])
        for kind in (B_R, B_D, B_S):
            drain(kind + g, b_s.at[g])
    drain(A_X, a_x)
    drain(B_X, b_x)

    @pl.when(my_batch >= 0)
    def _():
        @pl.loop(0, COLS // OUT)
        def _(c):
            sent = gathered.at[pl.ds(0, SHARDS - 1), :, pl.ds(pl.multiple_of(c * OUT, OUT), OUT)]
            pltpu.make_async_copy(sent, sent, ssend_sem.at[c]).wait()

    @pl.loop(0, MATS)
    def _(k):
        whole = ortho_out.at[k // MB, k % MB]
        pltpu.make_async_copy(whole, whole, srecv_sem.at[k // MB, k % MB]).wait()


PIECE = 4


def outputs(moment, ortho, weight, moment_out, update_out, weight_out):
    moment_out[...] = moment[...]
    scaled = (0.2 * math.sqrt(max(ROWS, COLS))) * ortho[...].astype(F32)
    update_out[...] = scaled
    weight_out[...] = (weight[...].astype(F32) - step_size * scaled).astype(BF16)


def body(grad_parts, momentum, weight):
    grads = grad_parts.reshape(4, 2, BATCHES, MB, BAND, COLS)
    a_block, b_block = (BATCHES, NA, BAND, COLS), (BATCHES, HB, BAND, COLS)
    x_block = (BATCHES, NB, BAND, COLS)

    def buf(*shape):
        return pltpu.VMEM(shape, BF16)

    moment, ortho = pl.pallas_call(
        kernel,
        out_shape=(
            jax.ShapeDtypeStruct((BATCHES, MB, BAND, COLS), F32),
            jax.ShapeDtypeStruct((BATCHES, MB, BAND, COLS), BF16),
        ),
        in_specs=[pl.BlockSpec(memory_space=pl.ANY)] * 2,
        out_specs=(pl.BlockSpec(memory_space=pl.ANY),) * 2,
        scratch_shapes=[
            pltpu.VMEM((BATCHES, MB, BAND, COLS), F32), pltpu.VMEM((BATCHES, MB, BAND, COLS), F32),
            buf(*a_block), buf(*a_block), buf(2, *a_block), buf(4, *x_block),
            buf(2, *a_block), buf(2, *a_block), buf(2, *a_block), buf(*a_block), buf(2, *a_block), buf(*a_block),
            buf(4, *x_block), buf(4, *x_block),
            buf(2, *b_block), buf(2, *b_block), buf(2, *b_block), buf(2, *b_block),
            buf(BATCHES, MB, BAND, COLS),
            buf(SHARDS, BAND, COLS),
            pltpu.VMEM((ROWS, ROWS), F32), pltpu.VMEM((ROWS, ROWS), BF16), pltpu.VMEM((8, 128), F32),
            pltpu.SemaphoreType.DMA((5,)),
            pltpu.SemaphoreType.DMA((KINDS,)), pltpu.SemaphoreType.DMA((KINDS, STEPS)),
            pltpu.SemaphoreType.DMA((BATCHES, MB)), pltpu.SemaphoreType.DMA((STEPS,)),
            pltpu.SemaphoreType.DMA((COLS // OUT,)), pltpu.SemaphoreType.DMA((BATCHES, MB)),
            pltpu.SemaphoreType.REGULAR((3,)), pltpu.SemaphoreType.DMA((STEPS,)),
        ],
        compiler_params=pltpu.CompilerParams(
            collective_id=0, has_side_effects=True, vmem_limit_bytes=56 * 1024 * 1024
        ),
        name="muon_step",
    )(grads, momentum.reshape(BATCHES, MB, BAND, COLS))
    block = pl.BlockSpec((PIECE, BAND, COLS), lambda i: (i, 0, 0))
    return tuple(
        pl.pallas_call(
            outputs,
            grid=(MATS // PIECE,),
            out_shape=(
                jax.ShapeDtypeStruct((MATS, BAND, COLS), F32),
                jax.ShapeDtypeStruct((MATS, BAND, COLS), F32),
                jax.ShapeDtypeStruct((MATS, BAND, COLS), BF16),
            ),
            in_specs=[block] * 3,
            out_specs=(block,) * 3,
            compiler_params=pltpu.CompilerParams(vmem_limit_bytes=56 * 1024 * 1024),
            name="outputs",
        )(moment.reshape(MATS, BAND, COLS), ortho.reshape(MATS, BAND, COLS), weight)
    )


def solution(mesh):
    return jax.shard_map(
        body,
        mesh=mesh,
        in_specs=(P("dp", None, "shard", None), P("dp", "shard", None), P("dp", "shard", None)),
        out_specs=(P("dp", "shard", None), P("dp", "shard", None), P("dp", "shard", None)),
        check_vma=False,
    )
```
